32 devices in a mesh: freq: 4 (over y, core), gx: 8 (over z, x).
Axes of the slice: x: 2, y: 2, z: 4, core: 2. Of those that a mesh axis runs over, the one named last changes fastest.
Arguments:
- sigma_h: float32 [32, 64, 256], P('gx'), may hold values from 0.3 to 3
- sigma_v: float32 [32, 64, 256], P('gx'), may hold values from 0.3 to 3
- wave_scale: float32 [4], P('freq'), may hold values from 0.25 to 4
- field_start: bfloat16 [4, 2, 3, 32, 64, 256], P('freq', None, None, 'gx'), may hold values from -6 to 6
- adjoint_start: bfloat16 [4, 2, 3, 32, 64, 256], P('freq', None, None, 'gx'), may hold values from -6 to 6
- observed: bfloat16 [4, 2, 3, 32, 64, 256], P('freq', None, None, 'gx'), may hold values from -6 to 6
- tx_count: int32 [1], replicated, may hold values from 1 to 64
- tx_cells: int32 [64], replicated, may hold values from 0 to 524287
Outputs:
- gradient: float32 [2, 32, 64, 256], P(None, 'gx', 'freq')
- final_field: float32 [4, 2, 3, 32, 64, 256], P('freq', None, None, 'gx')
The draws below stay inside these ranges and needn't reach their ends.
All inputs are finite; a program needn't handle non-finite values.
Results may differ from the reference program's by a relative error of at most 0.0003.
Values sent between devices are 32-bit elements; how exact they have to be, the bound alone decides.
A program may use at most 64 MiB of HBM per device.

```python
import math
import jax
import jax.numpy as jnp
from jax import lax

NY = 64
NZ = 256
ITERS = 2
TX_MAX = 64
FREQS = 4
NX = 32


def with_ends(array, rng, low, high):
    spot = [jax.random.randint(jax.random.fold_in(rng, axis), (), 0, length) for axis, length in enumerate(array.shape)]
    main_axis = array.shape.index(max(array.shape))
    next_to = spot[:main_axis] + [(spot[main_axis] + 1) % array.shape[main_axis]] + spot[main_axis + 1:]
    return array.at[tuple(spot)].set(low).at[tuple(next_to)].set(high)


def shard_levels(key, extent, pieces, low, high):
    def one(position, shards_of):
        heights = jax.random.uniform(jax.random.fold_in(jax.random.fold_in(key, 6), position), (shards_of,), jnp.float32, low / len(pieces), high / len(pieces))
        return jnp.repeat(jnp.exp(heights), extent[position] // shards_of).reshape((-1,) + (1,) * (len(extent) - position - 1))

    factor_of = one(*pieces[0])
    for cut in pieces[1:]:
        factor_of = factor_of * one(*cut)
    return factor_of


def normal_values(rng, extent, deviation, reach, pieces=(), kind=jnp.bfloat16):
    result = jax.random.normal(rng, extent, jnp.float32) * deviation
    if len(pieces) > 0:
        result = shard_levels(rng, extent, pieces, -0.22, 0.18) * result
    return jnp.clip(result, min=-reach, max=reach).astype(kind)


def setup_inputs(seed: int = 0) -> dict:
    keys = jax.random.split(jax.random.key(seed), 9)
    return {
        "sigma_h": jnp.clip(jnp.exp(math.log(3.0) - 2.3025851 * jax.random.uniform(keys[0], (NX, NY, NZ), jnp.float32) ** shard_levels(keys[0], (NX, NY, NZ), ((0, 8),), -0.2, 0.2)), 0.3, 3.0),
        "sigma_v": jnp.clip(jnp.exp(math.log(3.0) - 2.3025851 * jax.random.uniform(keys[1], (NX, NY, NZ), jnp.float32) ** shard_levels(keys[1], (NX, NY, NZ), ((0, 8),), -0.2, 0.2)), 0.3, 3.0),
        "wave_scale": jnp.clip(jnp.exp(math.log(4.0) - 2.7725887 * jax.random.uniform(keys[2], (FREQS,), jnp.float32) ** shard_levels(keys[2], (FREQS,), ((0, 4),), -0.2, 0.2)), 0.25, 4.0),
        "field_start": normal_values(keys[3], (FREQS, 2, 3, NX, NY, NZ), 1.0, 6.0, ((0, 4), (3, 8))),
        "adjoint_start": normal_values(keys[4], (FREQS, 2, 3, NX, NY, NZ), 1.0, 6.0, ((0, 4), (3, 8))),
        "observed": normal_values(keys[5], (FREQS, 2, 3, NX, NY, NZ), 1.0, 6.0, ((0, 4), (3, 8))),
        "tx_count": jax.random.randint(keys[6], (1,), 1, TX_MAX + 1).astype(jnp.int32),
        "tx_cells": with_ends(jax.random.randint(keys[7], (TX_MAX,), 0, NX * NY * NZ), jax.random.fold_in(keys[7], 1), 0, (NX * NY * NZ) - 1).astype(jnp.int32),
    }


THETA = 0.5
SOURCE_GAIN = 8.0


def ahead_diff(values, along):
    along = values.ndim + along
    widths = [(0, 0)] * values.ndim
    widths[along] = (0, 1)
    padded = jnp.pad(values, widths)
    return lax.slice_in_dim(padded, 1, values.shape[along] + 1, axis=along) - values


def behind_diff(values, along):
    along = values.ndim + along
    widths = [(0, 0)] * values.ndim
    widths[along] = (1, 0)
    padded = jnp.pad(values, widths)
    return values - lax.slice_in_dim(padded, 0, values.shape[along], axis=along)


def curl_curl(efield):
    comp_x = efield[..., 0, :, :, :]
    comp_y = efield[..., 1, :, :, :]
    comp_z = efield[..., 2, :, :, :]
    twist_x = ahead_diff(comp_z, -2) - ahead_diff(comp_y, -1)
    twist_y = ahead_diff(comp_x, -1) - ahead_diff(comp_z, -3)
    twist_z = ahead_diff(comp_y, -3) - ahead_diff(comp_x, -2)
    back_x = behind_diff(twist_z, -2) - behind_diff(twist_y, -1)
    back_y = behind_diff(twist_x, -1) - behind_diff(twist_z, -3)
    back_z = behind_diff(twist_y, -3) - behind_diff(twist_x, -2)
    return jnp.stack([back_x, back_y, back_z], axis=-4)


def relax(efield, curled, source_term, sig_pair, wave_scale):
    sigma_comp = jnp.stack([sig_pair[0], sig_pair[0], sig_pair[1]])
    coupling = wave_scale[:, None, None, None, None] * sigma_comp[None]
    real_part = efield[:, 0]
    imag_part = efield[:, 1]
    resid_real = source_term[:, 0] - (curled[:, 0] - coupling * imag_part)
    resid_imag = source_term[:, 1] - (curled[:, 1] + coupling * real_part)
    modulus = 16.0 + coupling * coupling
    update_real = (4.0 * resid_real + coupling * resid_imag) / modulus
    update_imag = (4.0 * resid_imag - coupling * resid_real) / modulus
    return efield + THETA * jnp.stack([update_real, update_imag], axis=1)


def make_source(tx_cells, tx_count, wave_scale, x_start, slab_width, size_y, size_z):
    plane_size = size_y * size_z
    cell_x = tx_cells // plane_size - x_start
    remainder = tx_cells % plane_size
    cell_y = remainder // size_z
    cell_z = remainder % size_z
    active = (jnp.arange(tx_cells.shape[0]) < tx_count[0]) & (cell_x >= 0) & (cell_x < slab_width)
    weights = jnp.where(active, 1.0, 0.0).astype(jnp.float32)
    counts = jnp.zeros((slab_width, size_y, size_z), jnp.float32)
    counts = counts.at[jnp.clip(cell_x, 0, slab_width - 1), cell_y, cell_z].add(weights)
    imag_x = SOURCE_GAIN * wave_scale[:, None, None, None] * counts[None]
    blank = jnp.zeros_like(imag_x)
    real_block = jnp.stack([blank, blank, blank], axis=1)
    imag_block = jnp.stack([imag_x, blank, blank], axis=1)
    return jnp.stack([real_block, imag_block], axis=1)


def adjoint_source(efield, observed):
    differ = efield - observed.astype(jnp.float32)
    return jnp.stack([differ[:, 0], -differ[:, 1]], axis=1)


def gradient_terms(efield, adjoint, wave_scale):
    product = adjoint[:, 0] * efield[:, 1] + adjoint[:, 1] * efield[:, 0]
    weighted = wave_scale[:, None, None, None, None] * product
    horizontal = jnp.sum(weighted[:, 0] + weighted[:, 1], axis=0)
    vertical = jnp.sum(weighted[:, 2], axis=0)
    return jnp.stack([horizontal, vertical])


def reference(sigma_h, sigma_v, wave_scale, field_start, adjoint_start, observed, tx_count, tx_cells):
    sig_pair = jnp.stack([sigma_h, sigma_v])

    def per_freq(gradient, inputs):
        wave_one, start_one, adjoint_one, observed_one = inputs
        wave_vec = wave_one[None]
        source_term = make_source(tx_cells, tx_count, wave_vec, 0, NX, NY, NZ)
        efield = start_one[None].astype(jnp.float32)
        for sweep in range(ITERS):
            efield = relax(efield, curl_curl(efield), source_term, sig_pair, wave_vec)
        adjoint_rhs = adjoint_source(efield, observed_one[None])
        adjoint = adjoint_one[None].astype(jnp.float32)
        for sweep in range(ITERS):
            adjoint = relax(adjoint, curl_curl(adjoint), adjoint_rhs, sig_pair, wave_vec)
        gradient = gradient + gradient_terms(efield, adjoint, wave_vec)
        return gradient, efield[0]

    initial = jnp.zeros((2, NX, NY, NZ), jnp.float32)
    gradient, fields = lax.scan(per_freq, initial, (wave_scale, field_start, adjoint_start, observed))
    return gradient, fields
```

```python
import functools

import jax
import jax.numpy as jnp
from jax import lax
from jax.experimental import pallas as pl
from jax.experimental.pallas import tpu as pltpu
from jax.sharding import PartitionSpec as P

THETA = 0.5
SOURCE_GAIN = 8.0
MESH = pl.DeviceIdType.MESH
E0, E1, A0, A1 = 0, 1, 2, 3


def sweeps_kernel(
    freqs, slabs, tx_max,
    sig_h, sig_v, wave, field_start, adjoint_start, observed, tx_count, tx_cells,
    grad_out, field,
    xs, yz, gs, coef, onehot_row, onehot_z, counts, grad_send, grad_recv,
    halo_send, halo_recv, peer_send, peer_recv,
):
    width, rows, cols = sig_h.shape
    share = rows // freqs
    last = width - 1
    me_f = lax.axis_index("freq")
    me_x = lax.axis_index("gx")
    has_left = me_x > 0
    has_right = me_x < slabs - 1
    scale = wave[0]
    row_id = lax.broadcasted_iota(jnp.int32, (rows, cols), 0)
    col_id = lax.broadcasted_iota(jnp.int32, (rows, cols), 1)

    def up_y(v):
        return jnp.where(row_id == rows - 1, 0.0, pltpu.roll(v, rows - 1, 0))

    def up_z(v):
        return jnp.where(col_id == cols - 1, 0.0, pltpu.roll(v, cols - 1, 1))

    def down_y(v):
        return jnp.where(row_id == 0, 0.0, pltpu.roll(v, 1, 0))

    def down_z(v):
        return jnp.where(col_id == 0, 0.0, pltpu.roll(v, 1, 1))

    def put(s, i, r, vx, vy, vz):
        xs[s, i, r] = vx
        yz[s, i, 0, r] = vy
        yz[s, i, 1, r] = vz
        gs[s, i + 1, 0, r] = vy + (up_y(vx) - vx)
        gs[s, i + 1, 1, r] = vz + (up_z(vx) - vx)

    def fill(s, i, start):
        for r in range(2):
            put(s, i, r, *(start[0, r, c, i].astype(jnp.float32) for c in range(3)))

    def ends(s):
        @pl.when(jnp.logical_not(has_left))
        def _():
            gs[s, 0] = yz[s, 0]

        @pl.when(jnp.logical_not(has_right))
        def _():
            yz[s, width] = jnp.zeros((2, 2, rows, cols), jnp.float32)

    def curl(s, i, r):
        vx, vy, vz = xs[s, i, r], yz[s, i, 0, r], yz[s, i, 1, r]
        hx = (up_y(vz) - vz) - (up_z(vy) - vy)
        hy = gs[s, i + 1, 1, r] - yz[s, i + 1, 1, r]
        hz = yz[s, i + 1, 0, r] - gs[s, i + 1, 0, r]
        hy_before = gs[s, i, 1, r] - vz
        hz_before = vy - gs[s, i, 0, r]
        kx = (hz - down_y(hz)) - (hy - down_z(hy))
        ky = (hx - down_z(hx)) - (hz - hz_before)
        kz = (hy - hy_before) - (hx - down_y(hx))
        return (vx, vy, vz), (kx, ky, kz)

    def update(s, i, rhs):
        real, k_real = curl(s, i, 0)
        imag, k_imag = curl(s, i, 1)
        out_re, out_im = [], []
        for c in range(3):
            which = 1 if c == 2 else 0
            coupling = scale * (sig_v if which else sig_h)[i]
            main, cross = coef[which, 0, i], coef[which, 1, i]
            b_re, b_im = rhs(c, i)
            r_re = b_re - (k_real[c] - coupling * imag[c])
            r_im = b_im - (k_imag[c] + coupling * real[c])
            out_re.append(real[c] + (main * r_re + cross * r_im))
            out_im.append(imag[c] + (main * r_im - cross * r_re))
        return out_re, out_im

    def source(c, i):
        return 0.0, (SOURCE_GAIN * scale) * counts[i] if c == 0 else 0.0

    def misfit(c, i):
        return (
            field[0, 0, c, i] - observed[0, 0, c, i].astype(jnp.float32),
            observed[0, 1, c, i].astype(jnp.float32) - field[0, 1, c, i],
        )

    def advance(s, i, rhs):
        out_re, out_im = update(s, i, rhs)
        put(s + 1, i, 0, *out_re)
        put(s + 1, i, 1, *out_im)

    def finish_field(i):
        out_re, out_im = update(E1, i, source)
        for c in range(3):
            field[0, 0, c, i] = out_re[c]
            field[0, 1, c, i] = out_im[c]

    def finish_grad(i, phase, slot):
        out_re, out_im = update(A1, i, misfit)
        terms = [
            scale * (out_re[c] * field[0, 1, c, i] + out_im[c] * field[0, 0, c, i])
            for c in range(3)
        ]
        for which, term in enumerate((terms[0] + terms[1], terms[2])):
            for f in range(freqs):
                grad_send[phase, f, which, slot] = term[f * share:(f + 1) * share]

    def rightward(s):
        return pltpu.make_async_remote_copy(
            gs.at[s, width], gs.at[s, 0], halo_send.at[s, 0], halo_recv.at[s, 0],
            device_id={"gx": me_x + 1}, device_id_type=MESH,
        )

    def leftward(s):
        return pltpu.make_async_remote_copy(
            yz.at[s, 0], yz.at[s, width], halo_send.at[s, 1], halo_recv.at[s, 1],
            device_id={"gx": me_x - 1}, device_id_type=MESH,
        )

    def send_right(s):
        pl.when(has_right)(lambda: rightward(s).start())

    def send_left(s):
        pl.when(has_left)(lambda: leftward(s).start())

    def wait_left(s):
        pl.when(has_left)(lambda: rightward(s).wait_recv())

    def wait_right(s):
        pl.when(has_right)(lambda: leftward(s).wait_recv())

    def to_peer(phase, off):
        peer = lax.rem(me_f + off, freqs)
        return pltpu.make_async_remote_copy(
            grad_send.at[phase, peer], grad_recv.at[phase, off],
            peer_send.at[phase, off], peer_recv.at[phase, off],
            device_id={"freq": peer}, device_id_type=MESH,
        )

    def inner(body):
        if width > 2:
            lax.fori_loop(1, last, lambda i, _: (body(i), 0)[1], 0)

    barrier = pltpu.get_barrier_semaphore()

    @pl.when(has_left)
    def _():
        pl.semaphore_signal(barrier, 1, device_id={"gx": me_x - 1}, device_id_type=MESH)

    @pl.when(has_right)
    def _():
        pl.semaphore_signal(barrier, 1, device_id={"gx": me_x + 1}, device_id_type=MESH)

    for off in range(1, freqs):
        pl.semaphore_signal(
            barrier, 1, device_id={"freq": lax.rem(me_f + off, freqs)}, device_id_type=MESH
        )
    fill(E0, 0, field_start)
    fill(E0, last, field_start)
    pl.semaphore_wait(
        barrier, freqs - 1 + has_left.astype(jnp.int32) + has_right.astype(jnp.int32)
    )
    send_left(E0)
    send_right(E0)
    ends(E0)
    fill(A0, 0, adjoint_start)
    fill(A0, last, adjoint_start)
    ends(A0)

    def prepare(i):
        for which, sig in enumerate((sig_h, sig_v)):
            coupling = scale * sig[i]
            part = THETA / (16.0 + coupling * coupling)
            coef[which, 0, i] = 4.0 * part
            coef[which, 1, i] = coupling * part

    lax.fori_loop(0, width, lambda i, _: (prepare(i), 0)[1], 0)

    row_line = lax.broadcasted_iota(jnp.int32, (1, width * rows), 1)
    col_line = lax.broadcasted_iota(jnp.int32, (1, cols), 1)

    def mark(t, _):
        cell = tx_cells[t]
        row = cell // cols
        col = cell - row * cols
        row = jnp.where(t < tx_count[0], row - me_x * (width * rows), -1)
        onehot_row[pl.ds(t, 1), :] = jnp.where(row_line == row, 1.0, 0.0)
        onehot_z[pl.ds(t, 1), :] = jnp.where(col_line == col, 1.0, 0.0)
        return 0

    lax.fori_loop(0, tx_max, mark, 0)
    counts[...] = lax.dot_general(
        onehot_row[...].astype(jnp.bfloat16), onehot_z[...].astype(jnp.bfloat16),
        (((0,), (0,)), ((), ())), preferred_element_type=jnp.float32,
    ).reshape(width, rows, cols)

    inner(lambda i: fill(E0, i, field_start))
    inner(lambda i: fill(A0, i, adjoint_start))
    inner(lambda i: advance(E0, i, source))

    wait_left(E0)
    send_left(A0)
    advance(E0, 0, source)
    send_left(E1)
    wait_right(E0)
    send_right(A0)
    advance(E0, last, source)
    send_right(E1)
    ends(E1)
    inner(finish_field)
    inner(lambda i: advance(A0, i, misfit))

    wait_left(E1)
    finish_field(0)
    wait_left(A0)
    advance(A0, 0, misfit)
    send_left(A1)
    wait_right(E1)
    finish_field(last)
    wait_right(A0)
    advance(A0, last, misfit)
    send_right(A1)
    ends(A1)

    if width > 2:
        lax.fori_loop(1, last, lambda i, _: (finish_grad(i, 0, i - 1), 0)[1], 0)
    for off in range(1, freqs):
        to_peer(0, off).start()
    wait_left(A1)
    finish_grad(0, 1, 0)
    wait_right(A1)
    finish_grad(last, 1, 1)
    for off in range(1, freqs):
        to_peer(1, off).start()

    for phase, layers in ((0, tuple(range(1, last))), (1, (0, last))):
        total = grad_send[phase, me_f]
        for off in range(1, freqs):
            to_peer(phase, off).wait_recv()
            total = total + grad_recv[phase, off]
        for slot, layer in enumerate(layers):
            grad_out[:, layer] = total[:, slot]
    for off in range(1, freqs):
        to_peer(0, off).wait_send()
        to_peer(1, off).wait_send()
    for s in (E0, E1, A0, A1):
        pl.when(has_right)(lambda: rightward(s).wait_send())
        pl.when(has_left)(lambda: leftward(s).wait_send())


def on_device(freqs, slabs, sigma_h, sigma_v, wave_scale, field_start, adjoint_start, observed, tx_count, tx_cells):
    width, rows, cols = sigma_h.shape
    tx_max = tx_cells.shape[0]
    share = rows // freqs
    inner_count = max(width - 2, 2)
    vmem = pl.BlockSpec(memory_space=pltpu.VMEM)
    smem = pl.BlockSpec(memory_space=pltpu.SMEM)
    f32 = jnp.float32
    return pl.pallas_call(
        functools.partial(sweeps_kernel, freqs, slabs, tx_max),
        out_shape=(
            jax.ShapeDtypeStruct((2, width, share, cols), f32),
            jax.ShapeDtypeStruct(field_start.shape, f32),
        ),
        in_specs=[vmem, vmem, smem, vmem, vmem, vmem, smem, smem],
        out_specs=(vmem, vmem),
        scratch_shapes=[
            pltpu.VMEM((4, width, 2, rows, cols), f32),
            pltpu.VMEM((4, width + 1, 2, 2, rows, cols), f32),
            pltpu.VMEM((4, width + 1, 2, 2, rows, cols), f32),
            pltpu.VMEM((2, 2, width, rows, cols), f32),
            pltpu.VMEM((tx_max, width * rows), f32),
            pltpu.VMEM((tx_max, cols), f32),
            pltpu.VMEM((width, rows, cols), f32),
            pltpu.VMEM((2, freqs, 2, inner_count, share, cols), f32),
            pltpu.VMEM((2, freqs, 2, inner_count, share, cols), f32),
            pltpu.SemaphoreType.DMA((4, 2)),
            pltpu.SemaphoreType.DMA((4, 2)),
            pltpu.SemaphoreType.DMA((2, freqs)),
            pltpu.SemaphoreType.DMA((2, freqs)),
        ],
        compiler_params=pltpu.CompilerParams(
            collective_id=0, has_side_effects=True, vmem_limit_bytes=48 * 1024 * 1024
        ),
    )(sigma_h, sigma_v, wave_scale, field_start, adjoint_start, observed, tx_count, tx_cells)


def solution(mesh):
    placed = (
        P("gx", None, None),
        P("gx", None, None),
        P("freq"),
        P("freq", None, None, "gx", None, None),
        P("freq", None, None, "gx", None, None),
        P("freq", None, None, "gx", None, None),
        P(),
        P(),
    )
    return jax.shard_map(
        functools.partial(on_device, mesh.shape["freq"], mesh.shape["gx"]),
        mesh=mesh,
        in_specs=placed,
        out_specs=(P(None, "gx", "freq", None), P("freq", None, None, "gx", None, None)),
        check_vma=False,
    )
```

```python
import functools

import jax
import jax.numpy as jnp
from jax import lax
from jax.experimental import pallas as pl
from jax.experimental.pallas import tpu as pltpu
from jax.sharding import PartitionSpec as P

THETA = 0.5
SOURCE_GAIN = 8.0
MESH = pl.DeviceIdType.MESH
E0, E1, A0, A1 = 0, 1, 2, 3


def sweeps_kernel(
    freqs, slabs, tx_max,
    sig_h_in, sig_v_in, wave, field_in, adjoint_in, observed_in, tx_count, tx_cells,
    grad_out, field,
    sig_h, sig_v, field_start, adjoint_start, observed,
    xs, yz, gs, coef, onehot_row, onehot_z, counts, grad_send, grad_recv,
    load_sem, halo_send, halo_recv, peer_send, peer_recv,
):
    width, rows, cols = sig_h.shape
    share = rows // freqs
    last = width - 1
    half = rows // 2
    early = half - 8
    whole = (0, rows)
    cut = {E0: (early, early - 8), E1: (early, early), A0: (early, early), A1: (half, early)}
    me_f = lax.axis_index("freq")
    me_x = lax.axis_index("gx")
    has_left = me_x > 0
    has_right = me_x < slabs - 1
    scale = wave[0]

    def up_y(v, top):
        moved = pltpu.roll(v, v.shape[0] - 1, 0)
        if not top:
            return moved
        row_id = lax.broadcasted_iota(jnp.int32, v.shape, 0)
        return jnp.where(row_id == v.shape[0] - 1, 0.0, moved)

    def down_y(v, bottom):
        moved = pltpu.roll(v, 1, 0)
        if not bottom:
            return moved
        return jnp.where(lax.broadcasted_iota(jnp.int32, v.shape, 0) == 0, 0.0, moved)

    def up_z(v):
        col_id = lax.broadcasted_iota(jnp.int32, v.shape, 1)
        return jnp.where(col_id == cols - 1, 0.0, pltpu.roll(v, cols - 1, 1))

    def down_z(v):
        col_id = lax.broadcasted_iota(jnp.int32, v.shape, 1)
        return jnp.where(col_id == 0, 0.0, pltpu.roll(v, 1, 1))

    def put(s, i, r, part, vx, vy, vz):
        lo, hi = part
        xs[s, i, r, lo:hi] = vx
        yz[s, i, 0, r, lo:hi] = vy
        yz[s, i, 1, r, lo:hi] = vz
        if hi == rows:
            above = up_y(vx, True)
        else:
            above = up_y(xs[s, i, r, lo:hi + 8], False)[:hi - lo]
        gs[s, i + 1, 0, r, lo:hi] = vy + (above - vx)
        gs[s, i + 1, 1, r, lo:hi] = vz + (up_z(vx) - vx)

    def fill(s, i, start):
        for r in range(2):
            put(s, i, r, whole, *(start[r, c, i].astype(jnp.float32) for c in range(3)))

    def left_end(s, part):
        lo, hi = part

        @pl.when(jnp.logical_not(has_left))
        def _():
            gs[s, 0, :, :, lo:hi] = yz[s, 0, :, :, lo:hi]

    def curl(s, i, r, part):
        lo, hi = part
        w0, w1 = max(lo - 8, 0), min(hi + 8, rows)

        def crop(v):
            return v[lo - w0:hi - w0]

        vx = xs[s, i, r, lo:hi]
        wide_y, wide_z = yz[s, i, 0, r, w0:w1], yz[s, i, 1, r, w0:w1]
        hx = (up_y(wide_z, w1 == rows) - wide_z) - (up_z(wide_y) - wide_y)
        hz = yz[s, i + 1, 0, r, w0:w1] - gs[s, i + 1, 0, r, w0:w1]
        hy = gs[s, i + 1, 1, r, lo:hi] - yz[s, i + 1, 1, r, lo:hi]
        vy, vz = crop(wide_y), crop(wide_z)
        hy_before = gs[s, i, 1, r, lo:hi] - vz
        hz_before = vy - gs[s, i, 0, r, lo:hi]
        hx_c, hz_c = crop(hx), crop(hz)
        kx = (hz_c - crop(down_y(hz, w0 == 0))) - (hy - down_z(hy))
        ky = (hx_c - down_z(hx_c)) - (hz_c - hz_before)
        kz = (hy - hy_before) - (hx_c - crop(down_y(hx, w0 == 0)))
        return (vx, vy, vz), (kx, ky, kz)

    def update(s, i, rhs, part):
        lo, hi = part
        real, k_real = curl(s, i, 0, part)
        imag, k_imag = curl(s, i, 1, part)
        out_re, out_im = [], []
        for c in range(3):
            which = 1 if c == 2 else 0
            coupling = scale * (sig_v if which else sig_h)[i, lo:hi]
            main, cross = coef[which, 0, i, lo:hi], coef[which, 1, i, lo:hi]
            b_re, b_im = rhs(c, i, part)
            r_re = b_re - (k_real[c] - coupling * imag[c])
            r_im = b_im - (k_imag[c] + coupling * real[c])
            out_re.append(real[c] + (main * r_re + cross * r_im))
            out_im.append(imag[c] + (main * r_im - cross * r_re))
        return out_re, out_im

    def source(c, i, part):
        lo, hi = part
        return 0.0, (SOURCE_GAIN * scale) * counts[i, lo:hi] if c == 0 else 0.0

    def misfit(c, i, part):
        lo, hi = part
        from_row = lo // 16 * 16
        to_row = (hi + 15) // 16 * 16
        seen = [
            observed[r, c, i, from_row:to_row].astype(jnp.float32)[lo - from_row:hi - from_row]
            for r in range(2)
        ]
        return field[0, 0, c, i, lo:hi] - seen[0], seen[1] - field[0, 1, c, i, lo:hi]

    def advance(s, i, rhs, part=whole):
        out_re, out_im = update(s, i, rhs, part)
        put(s + 1, i, 0, part, *out_re)
        put(s + 1, i, 1, part, *out_im)

    def finish_field(i, part=whole):
        lo, hi = part
        out_re, out_im = update(E1, i, source, part)
        for c in range(3):
            field[0, 0, c, i, lo:hi] = out_re[c]
            field[0, 1, c, i, lo:hi] = out_im[c]

    def finish_grad(i, phase, slot, part=whole):
        lo, hi = part
        out_re, out_im = update(A1, i, misfit, part)
        terms = [
            scale * (out_re[c] * field[0, 1, c, i, lo:hi] + out_im[c] * field[0, 0, c, i, lo:hi])
            for c in range(3)
        ]
        for which, term in enumerate((terms[0] + terms[1], terms[2])):
            for f in range(lo // share, hi // share):
                at = f * share - lo
                grad_send[phase, f, which, slot] = term[at:at + share]

    def piece(s, way, k):
        edge = cut[s][way]
        return pl.ds(edge, rows - edge) if k == 0 else pl.ds(0, edge)

    def rightward(s, k):
        at = piece(s, 0, k)
        return pltpu.make_async_remote_copy(
            gs.at[s, width, :, :, at], gs.at[s, 0, :, :, at],
            halo_send.at[s, 0, k], halo_recv.at[s, 0, k],
            device_id={"gx": me_x + 1}, device_id_type=MESH,
        )

    def leftward(s, k):
        at = piece(s, 1, k)
        return pltpu.make_async_remote_copy(
            yz.at[s, 0, :, :, at], yz.at[s, width, :, :, at],
            halo_send.at[s, 1, k], halo_recv.at[s, 1, k],
            device_id={"gx": me_x - 1}, device_id_type=MESH,
        )

    def send_right(s, k):
        pl.when(has_right)(lambda: rightward(s, k).start())

    def send_left(s, k):
        pl.when(has_left)(lambda: leftward(s, k).start())

    def wait_left(s, k):
        pl.when(has_left)(lambda: rightward(s, k).wait_recv())

    def wait_right(s, k):
        pl.when(has_right)(lambda: leftward(s, k).wait_recv())

    def to_peer(phase, off):
        peer = lax.rem(me_f + off, freqs)
        return pltpu.make_async_remote_copy(
            grad_send.at[phase, peer], grad_recv.at[phase, off],
            peer_send.at[phase, off], peer_recv.at[phase, off],
            device_id={"freq": peer}, device_id_type=MESH,
        )

    def inner(body):
        if width > 2:
            lax.fori_loop(1, last, lambda i, _: (body(i), 0)[1], 0)

    loads = [
        pltpu.make_async_copy(src, dst, load_sem.at[n])
        for n, (src, dst) in enumerate((
            (field_in.at[0, :, :, 0], field_start.at[:, :, 0]),
            (field_in.at[0, :, :, last], field_start.at[:, :, last]),
            (field_in.at[0, :, :, pl.ds(1, last - 1)], field_start.at[:, :, pl.ds(1, last - 1)]),
            (sig_h_in, sig_h),
            (sig_v_in, sig_v),
            (adjoint_in.at[0], adjoint_start),
            (observed_in.at[0], observed),
        ))
    ]
    for load in loads:
        load.start()
    barrier = pltpu.get_barrier_semaphore()

    @pl.when(has_left)
    def _():
        pl.semaphore_signal(barrier, 1, device_id={"gx": me_x - 1}, device_id_type=MESH)

    @pl.when(has_right)
    def _():
        pl.semaphore_signal(barrier, 1, device_id={"gx": me_x + 1}, device_id_type=MESH)

    for off in range(1, freqs):
        pl.semaphore_signal(
            barrier, 1, device_id={"freq": lax.rem(me_f + off, freqs)}, device_id_type=MESH
        )
    loads[0].wait()
    fill(E0, 0, field_start)
    loads[1].wait()
    fill(E0, last, field_start)
    pl.semaphore_wait(
        barrier, freqs - 1 + has_left.astype(jnp.int32) + has_right.astype(jnp.int32)
    )
    for k in range(2):
        send_left(E0, k)
        send_right(E0, k)

    @pl.when(jnp.logical_not(has_right))
    def _():
        for s in (E0, E1, A0, A1):
            yz[s, width] = jnp.zeros((2, 2, rows, cols), jnp.float32)

    left_end(E0, whole)
    for load in loads[2:]:
        load.wait()

    def prepare(i):
        for which, sig in enumerate((sig_h, sig_v)):
            coupling = scale * sig[i]
            part = THETA / (16.0 + coupling * coupling)
            coef[which, 0, i] = 4.0 * part
            coef[which, 1, i] = coupling * part

    lax.fori_loop(0, width, lambda i, _: (prepare(i), 0)[1], 0)

    row_line = lax.broadcasted_iota(jnp.int32, (1, width * rows), 1)
    col_line = lax.broadcasted_iota(jnp.int32, (1, cols), 1)

    def mark(t, _):
        cell = tx_cells[t]
        row = cell // cols
        col = cell - row * cols
        row = jnp.where(t < tx_count[0], row - me_x * (width * rows), -1)
        onehot_row[pl.ds(t, 1), :] = jnp.where(row_line == row, 1.0, 0.0)
        onehot_z[pl.ds(t, 1), :] = jnp.where(col_line == col, 1.0, 0.0)
        return 0

    lax.fori_loop(0, tx_max, mark, 0)
    counts[...] = lax.dot_general(
        onehot_row[...].astype(jnp.bfloat16), onehot_z[...].astype(jnp.bfloat16),
        (((0,), (0,)), ((), ())), preferred_element_type=jnp.float32,
    ).reshape(width, rows, cols)

    inner(lambda i: fill(E0, i, field_start))
    fill(A0, 0, adjoint_start)
    fill(A0, last, adjoint_start)
    left_end(A0, whole)

    for k, part in enumerate(((early, rows), (0, early))):
        wait_left(E0, k)
        if k == 0:
            send_left(A0, 0)
        advance(E0, 0, source, part)
        send_left(E1, k)
        left_end(E1, part)
        wait_right(E0, k)
        if k == 0:
            send_right(A0, 0)
        advance(E0, last, source, part)
        send_right(E1, k)
        if k == 0:
            send_left(A0, 1)
            send_right(A0, 1)
            inner(lambda i: advance(E0, i, source))
            inner(lambda i: fill(A0, i, adjoint_start))

    inner(finish_field)
    inner(lambda i: advance(A0, i, misfit))

    for k, (near, far) in enumerate((((early, rows), (half, rows)), ((0, early), (0, half)))):
        wait_left(E1, k)
        finish_field(0, near)
        wait_left(A0, k)
        advance(A0, 0, misfit, near)
        send_left(A1, k)
        left_end(A1, near)
        wait_right(E1, k)
        finish_field(last, far)
        wait_right(A0, k)
        advance(A0, last, misfit, far)
        send_right(A1, k)

    if width > 2:
        lax.fori_loop(1, last, lambda i, _: (finish_grad(i, 0, i - 1), 0)[1], 0)
    for off in range(1, freqs):
        to_peer(0, off).start()
    for k, part in enumerate(((half, rows), (0, half))):
        wait_left(A1, k)
        finish_grad(0, 1, 0, part)
        wait_right(A1, k)
        finish_grad(last, 1, 1, part)
        for off in range(1, freqs):
            upper = lax.rem(me_f + off, freqs) >= freqs // 2
            pl.when(upper if k == 0 else jnp.logical_not(upper))(
                lambda: to_peer(1, off).start()
            )

    for phase, layers in ((0, tuple(range(1, last))), (1, (0, last))):
        total = grad_send[phase, me_f]
        for off in range(1, freqs):
            to_peer(phase, off).wait_recv()
            total = total + grad_recv[phase, off]
        for slot, layer in enumerate(layers):
            grad_out[:, layer] = total[:, slot]
    for off in range(1, freqs):
        to_peer(0, off).wait_send()
        to_peer(1, off).wait_send()
    for s in (E0, E1, A0, A1):
        for k in range(2):
            pl.when(has_right)(lambda: rightward(s, k).wait_send())
            pl.when(has_left)(lambda: leftward(s, k).wait_send())


def on_device(freqs, slabs, sigma_h, sigma_v, wave_scale, field_start, adjoint_start, observed, tx_count, tx_cells):
    width, rows, cols = sigma_h.shape
    tx_max = tx_cells.shape[0]
    share = rows // freqs
    inner_count = max(width - 2, 2)
    vmem = pl.BlockSpec(memory_space=pltpu.VMEM)
    hbm = pl.BlockSpec(memory_space=pltpu.HBM)
    smem = pl.BlockSpec(memory_space=pltpu.SMEM)
    f32 = jnp.float32
    return pl.pallas_call(
        functools.partial(sweeps_kernel, freqs, slabs, tx_max),
        out_shape=(
            jax.ShapeDtypeStruct((2, width, share, cols), f32),
            jax.ShapeDtypeStruct(field_start.shape, f32),
        ),
        in_specs=[hbm, hbm, smem, hbm, hbm, hbm, smem, smem],
        out_specs=(vmem, vmem),
        scratch_shapes=[
            pltpu.VMEM(sigma_h.shape, f32),
            pltpu.VMEM(sigma_v.shape, f32),
            pltpu.VMEM(field_start.shape[1:], field_start.dtype),
            pltpu.VMEM(adjoint_start.shape[1:], adjoint_start.dtype),
            pltpu.VMEM(observed.shape[1:], observed.dtype),
            pltpu.VMEM((4, width, 2, rows, cols), f32),
            pltpu.VMEM((4, width + 1, 2, 2, rows, cols), f32),
            pltpu.VMEM((4, width + 1, 2, 2, rows, cols), f32),
            pltpu.VMEM((2, 2, width, rows, cols), f32),
            pltpu.VMEM((tx_max, width * rows), f32),
            pltpu.VMEM((tx_max, cols), f32),
            pltpu.VMEM((width, rows, cols), f32),
            pltpu.VMEM((2, freqs, 2, inner_count, share, cols), f32),
            pltpu.VMEM((2, freqs, 2, inner_count, share, cols), f32),
            pltpu.SemaphoreType.DMA((7,)),
            pltpu.SemaphoreType.DMA((4, 2, 2)),
            pltpu.SemaphoreType.DMA((4, 2, 2)),
            pltpu.SemaphoreType.DMA((2, freqs)),
            pltpu.SemaphoreType.DMA((2, freqs)),
        ],
        compiler_params=pltpu.CompilerParams(
            collective_id=0, has_side_effects=True, vmem_limit_bytes=48 * 1024 * 1024
        ),
    )(sigma_h, sigma_v, wave_scale, field_start, adjoint_start, observed, tx_count, tx_cells)


def solution(mesh):
    placed = (
        P("gx", None, None),
        P("gx", None, None),
        P("freq"),
        P("freq", None, None, "gx", None, None),
        P("freq", None, None, "gx", None, None),
        P("freq", None, None, "gx", None, None),
        P(),
        P(),
    )
    return jax.shard_map(
        functools.partial(on_device, mesh.shape["freq"], mesh.shape["gx"]),
        mesh=mesh,
        in_specs=placed,
        out_specs=(P(None, "gx", "freq", None), P("freq", None, None, "gx", None, None)),
        check_vma=False,
    )
```

```python
import functools

import jax
import jax.numpy as jnp
from jax import lax
from jax.experimental import pallas as pl
from jax.experimental.pallas import tpu as pltpu
from jax.sharding import PartitionSpec as P

THETA = 0.5
SOURCE_GAIN = 8.0
MESH = pl.DeviceIdType.MESH
E0, E1, A0, A1 = 0, 1, 2, 3


def sweeps_kernel(
    freqs, slabs, tx_max,
    sig_h_in, sig_v_in, wave, field_in, adjoint_in, observed_in, tx_count, tx_cells,
    grad_hbm, field_hbm,
    grad_out, field, sig_h, sig_v, field_start, adjoint_start, observed,
    xs, yz, gs, coef, onehot_row, onehot_z, counts, grad_send, grad_recv,
    load_sem, store_sem, halo_send, halo_recv, peer_send, peer_recv,
):
    width, rows, cols = sig_h.shape
    share = rows // freqs
    last = width - 1
    half = rows // 2
    early = half - 8
    whole = (0, rows)
    low = half // 2
    cut = {
        E0: ((early, 0), (early - 8, 0)),
        E1: ((early, 0), (early, 0)),
        A0: ((early, 0), (early, 0)),
        A1: ((half, low, 0), (early, low - 8, 0)),
    }
    me_f = lax.axis_index("freq")
    me_x = lax.axis_index("gx")
    has_left = me_x > 0
    has_right = me_x < slabs - 1
    scale = wave[0]

    def up_y(v, top):
        moved = pltpu.roll(v, v.shape[0] - 1, 0)
        if not top:
            return moved
        row_id = lax.broadcasted_iota(jnp.int32, v.shape, 0)
        return jnp.where(row_id == v.shape[0] - 1, 0.0, moved)

    def down_y(v, bottom):
        moved = pltpu.roll(v, 1, 0)
        if not bottom:
            return moved
        return jnp.where(lax.broadcasted_iota(jnp.int32, v.shape, 0) == 0, 0.0, moved)

    def up_z(v):
        col_id = lax.broadcasted_iota(jnp.int32, v.shape, 1)
        return jnp.where(col_id == cols - 1, 0.0, pltpu.roll(v, cols - 1, 1))

    def down_z(v):
        col_id = lax.broadcasted_iota(jnp.int32, v.shape, 1)
        return jnp.where(col_id == 0, 0.0, pltpu.roll(v, 1, 1))

    def put(s, i, r, part, vx, vy, vz):
        lo, hi = part
        xs[s, i, r, lo:hi] = vx
        yz[s, i, 0, r, lo:hi] = vy
        yz[s, i, 1, r, lo:hi] = vz
        if hi == rows:
            above = up_y(vx, True)
        else:
            above = up_y(xs[s, i, r, lo:hi + 8], False)[:hi - lo]
        gs[s, i + 1, 0, r, lo:hi] = vy + (above - vx)
        gs[s, i + 1, 1, r, lo:hi] = vz + (up_z(vx) - vx)

    def fill(s, i, start):
        for r in range(2):
            put(s, i, r, whole, *(start[r, c, i].astype(jnp.float32) for c in range(3)))

    def left_end(s, part):
        lo, hi = part

        @pl.when(jnp.logical_not(has_left))
        def _():
            gs[s, 0, :, :, lo:hi] = yz[s, 0, :, :, lo:hi]

    def curl(s, i, r, part):
        lo, hi = part
        w0, w1 = max(lo - 8, 0), min(hi + 8, rows)

        def crop(v):
            return v[lo - w0:hi - w0]

        vx = xs[s, i, r, lo:hi]
        wide_y, wide_z = yz[s, i, 0, r, w0:w1], yz[s, i, 1, r, w0:w1]
        hx = (up_y(wide_z, w1 == rows) - wide_z) - (up_z(wide_y) - wide_y)
        hz = yz[s, i + 1, 0, r, w0:w1] - gs[s, i + 1, 0, r, w0:w1]
        hy = gs[s, i + 1, 1, r, lo:hi] - yz[s, i + 1, 1, r, lo:hi]
        vy, vz = crop(wide_y), crop(wide_z)
        hy_before = gs[s, i, 1, r, lo:hi] - vz
        hz_before = vy - gs[s, i, 0, r, lo:hi]
        hx_c, hz_c = crop(hx), crop(hz)
        kx = (hz_c - crop(down_y(hz, w0 == 0))) - (hy - down_z(hy))
        ky = (hx_c - down_z(hx_c)) - (hz_c - hz_before)
        kz = (hy - hy_before) - (hx_c - crop(down_y(hx, w0 == 0)))
        return (vx, vy, vz), (kx, ky, kz)

    def update(s, i, rhs, part):
        lo, hi = part
        real, k_real = curl(s, i, 0, part)
        imag, k_imag = curl(s, i, 1, part)
        out_re, out_im = [], []
        for c in range(3):
            which = 1 if c == 2 else 0
            coupling = scale * (sig_v if which else sig_h)[i, lo:hi]
            main, cross = coef[which, 0, i, lo:hi], coef[which, 1, i, lo:hi]
            b_re, b_im = rhs(c, i, part)
            r_re = b_re - (k_real[c] - coupling * imag[c])
            r_im = b_im - (k_imag[c] + coupling * real[c])
            out_re.append(real[c] + (main * r_re + cross * r_im))
            out_im.append(imag[c] + (main * r_im - cross * r_re))
        return out_re, out_im

    def source(c, i, part):
        lo, hi = part
        return 0.0, (SOURCE_GAIN * scale) * counts[i, lo:hi] if c == 0 else 0.0

    def misfit(c, i, part):
        lo, hi = part
        from_row = lo // 16 * 16
        to_row = (hi + 15) // 16 * 16
        seen = [
            observed[r, c, i, from_row:to_row].astype(jnp.float32)[lo - from_row:hi - from_row]
            for r in range(2)
        ]
        return field[0, c, i, lo:hi] - seen[0], seen[1] - field[1, c, i, lo:hi]

    def advance(s, i, rhs, part=whole):
        out_re, out_im = update(s, i, rhs, part)
        put(s + 1, i, 0, part, *out_re)
        put(s + 1, i, 1, part, *out_im)

    def finish_field(i, part=whole):
        lo, hi = part
        out_re, out_im = update(E1, i, source, part)
        for c in range(3):
            field[0, c, i, lo:hi] = out_re[c]
            field[1, c, i, lo:hi] = out_im[c]

    def finish_grad(i, phase, slot, part=whole):
        lo, hi = part
        out_re, out_im = update(A1, i, misfit, part)
        terms = [
            scale * (out_re[c] * field[1, c, i, lo:hi] + out_im[c] * field[0, c, i, lo:hi])
            for c in range(3)
        ]
        for which, term in enumerate((terms[0] + terms[1], terms[2])):
            for f in range(lo // share, hi // share):
                at = f * share - lo
                grad_send[phase, f, which, slot] = term[at:at + share]

    def piece(s, way, k):
        edges = (rows,) + cut[s][way]
        return pl.ds(edges[k + 1], edges[k] - edges[k + 1])

    def rightward(s, k):
        at = piece(s, 0, k)
        return pltpu.make_async_remote_copy(
            gs.at[s, width, :, :, at], gs.at[s, 0, :, :, at],
            halo_send.at[s, 0, k], halo_recv.at[s, 0, k],
            device_id={"gx": me_x + 1}, device_id_type=MESH,
        )

    def leftward(s, k):
        at = piece(s, 1, k)
        return pltpu.make_async_remote_copy(
            yz.at[s, 0, :, :, at], yz.at[s, width, :, :, at],
            halo_send.at[s, 1, k], halo_recv.at[s, 1, k],
            device_id={"gx": me_x - 1}, device_id_type=MESH,
        )

    def send_right(s, k):
        pl.when(has_right)(lambda: rightward(s, k).start())

    def send_left(s, k):
        pl.when(has_left)(lambda: leftward(s, k).start())

    def wait_left(s, k):
        pl.when(has_left)(lambda: rightward(s, k).wait_recv())

    def wait_right(s, k):
        pl.when(has_right)(lambda: leftward(s, k).wait_recv())

    def to_peer(phase, off):
        peer = lax.rem(me_f + off, freqs)
        return pltpu.make_async_remote_copy(
            grad_send.at[phase, peer], grad_recv.at[phase, off],
            peer_send.at[phase, off], peer_recv.at[phase, off],
            device_id={"freq": peer}, device_id_type=MESH,
        )

    def inner(body):
        if width > 2:
            lax.fori_loop(1, last, lambda i, _: (body(i), 0)[1], 0)

    loads = [
        pltpu.make_async_copy(src, dst, load_sem.at[n])
        for n, (src, dst) in enumerate((
            (field_in.at[0, :, :, 0], field_start.at[:, :, 0]),
            (field_in.at[0, :, :, last], field_start.at[:, :, last]),
            (field_in.at[0, :, :, pl.ds(1, last - 1)], field_start.at[:, :, pl.ds(1, last - 1)]),
            (sig_h_in, sig_h),
            (sig_v_in, sig_v),
            (adjoint_in.at[0], adjoint_start),
            (observed_in.at[0], observed),
        ))
    ]
    for load in loads:
        load.start()
    barrier = pltpu.get_barrier_semaphore()

    @pl.when(has_left)
    def _():
        pl.semaphore_signal(barrier, 1, device_id={"gx": me_x - 1}, device_id_type=MESH)

    @pl.when(has_right)
    def _():
        pl.semaphore_signal(barrier, 1, device_id={"gx": me_x + 1}, device_id_type=MESH)

    for off in range(1, freqs):
        pl.semaphore_signal(
            barrier, 1, device_id={"freq": lax.rem(me_f + off, freqs)}, device_id_type=MESH
        )
    loads[0].wait()
    fill(E0, 0, field_start)
    loads[1].wait()
    fill(E0, last, field_start)
    pl.semaphore_wait(
        barrier, freqs - 1 + has_left.astype(jnp.int32) + has_right.astype(jnp.int32)
    )
    for k in range(2):
        send_left(E0, k)
        send_right(E0, k)

    @pl.when(jnp.logical_not(has_right))
    def _():
        for s in (E0, E1, A0, A1):
            yz[s, width] = jnp.zeros((2, 2, rows, cols), jnp.float32)

    left_end(E0, whole)
    for load in loads[2:]:
        load.wait()

    def prepare(i):
        for which, sig in enumerate((sig_h, sig_v)):
            coupling = scale * sig[i]
            part = THETA / (16.0 + coupling * coupling)
            coef[which, 0, i] = 4.0 * part
            coef[which, 1, i] = coupling * part

    lax.fori_loop(0, width, lambda i, _: (prepare(i), 0)[1], 0)

    row_line = lax.broadcasted_iota(jnp.int32, (1, width * rows), 1)
    col_line = lax.broadcasted_iota(jnp.int32, (1, cols), 1)

    def mark(t, _):
        cell = tx_cells[t]
        row = cell // cols
        col = cell - row * cols
        row = jnp.where(t < tx_count[0], row - me_x * (width * rows), -1)
        onehot_row[pl.ds(t, 1), :] = jnp.where(row_line == row, 1.0, 0.0)
        onehot_z[pl.ds(t, 1), :] = jnp.where(col_line == col, 1.0, 0.0)
        return 0

    lax.fori_loop(0, tx_max, mark, 0)
    counts[...] = lax.dot_general(
        onehot_row[...].astype(jnp.bfloat16), onehot_z[...].astype(jnp.bfloat16),
        (((0,), (0,)), ((), ())), preferred_element_type=jnp.float32,
    ).reshape(width, rows, cols)

    inner(lambda i: fill(E0, i, field_start))
    fill(A0, 0, adjoint_start)
    fill(A0, last, adjoint_start)
    left_end(A0, whole)

    for k, part in enumerate(((early, rows), (0, early))):
        wait_left(E0, k)
        if k == 0:
            send_left(A0, 0)
        advance(E0, 0, source, part)
        send_left(E1, k)
        left_end(E1, part)
        wait_right(E0, k)
        if k == 0:
            send_right(A0, 0)
        advance(E0, last, source, part)
        send_right(E1, k)
        if k == 0:
            send_left(A0, 1)
            send_right(A0, 1)
            inner(lambda i: advance(E0, i, source))
            inner(lambda i: fill(A0, i, adjoint_start))

    inner(finish_field)
    inner(lambda i: advance(A0, i, misfit))

    for k, (near, far) in enumerate((((early, rows), (half, rows)), ((0, early), (0, half)))):
        wait_left(E1, k)
        finish_field(0, near)
        wait_left(A0, k)
        advance(A0, 0, misfit, near)
        for n in ((0,), (1, 2))[k]:
            send_left(A1, n)
        left_end(A1, near)
        wait_right(E1, k)
        finish_field(last, far)
        wait_right(A0, k)
        advance(A0, last, misfit, far)
        for n in ((0,), (1, 2))[k]:
            send_right(A1, n)

    store_field = pltpu.make_async_copy(field, field_hbm.at[0], store_sem.at[0])
    store_field.start()
    if width > 2:
        lax.fori_loop(1, last, lambda i, _: (finish_grad(i, 0, i - 1), 0)[1], 0)
    for off in range(1, freqs):
        to_peer(0, off).start()
    for k, part in enumerate(((half, rows), (low, half), (0, low))):
        wait_left(A1, k)
        finish_grad(0, 1, 0, part)
        wait_right(A1, k)
        finish_grad(last, 1, 1, part)
        for off in range(1, freqs):
            row = lax.rem(me_f + off, freqs) * share
            pl.when(jnp.logical_and(row >= part[0], row < part[1]))(
                lambda: to_peer(1, off).start()
            )

    for phase, layers in ((0, tuple(range(1, last))), (1, (0, last))):
        total = grad_send[phase, me_f]
        for off in range(1, freqs):
            to_peer(phase, off).wait_recv()
            total = total + grad_recv[phase, off]
        for slot, layer in enumerate(layers):
            grad_out[:, layer] = total[:, slot]
    store_grad = pltpu.make_async_copy(grad_out, grad_hbm, store_sem.at[1])
    store_grad.start()
    for off in range(1, freqs):
        to_peer(0, off).wait_send()
        to_peer(1, off).wait_send()
    for s in (E0, E1, A0, A1):
        for k in range(len(cut[s][0])):
            pl.when(has_right)(lambda: rightward(s, k).wait_send())
            pl.when(has_left)(lambda: leftward(s, k).wait_send())
    store_field.wait()
    store_grad.wait()


def on_device(freqs, slabs, sigma_h, sigma_v, wave_scale, field_start, adjoint_start, observed, tx_count, tx_cells):
    width, rows, cols = sigma_h.shape
    tx_max = tx_cells.shape[0]
    share = rows // freqs
    inner_count = max(width - 2, 2)
    hbm = pl.BlockSpec(memory_space=pltpu.HBM)
    smem = pl.BlockSpec(memory_space=pltpu.SMEM)
    f32 = jnp.float32
    return pl.pallas_call(
        functools.partial(sweeps_kernel, freqs, slabs, tx_max),
        out_shape=(
            jax.ShapeDtypeStruct((2, width, share, cols), f32),
            jax.ShapeDtypeStruct(field_start.shape, f32),
        ),
        in_specs=[hbm, hbm, smem, hbm, hbm, hbm, smem, smem],
        out_specs=(hbm, hbm),
        scratch_shapes=[
            pltpu.VMEM((2, width, share, cols), f32),
            pltpu.VMEM(field_start.shape[1:], f32),
            pltpu.VMEM(sigma_h.shape, f32),
            pltpu.VMEM(sigma_v.shape, f32),
            pltpu.VMEM(field_start.shape[1:], field_start.dtype),
            pltpu.VMEM(adjoint_start.shape[1:], adjoint_start.dtype),
            pltpu.VMEM(observed.shape[1:], observed.dtype),
            pltpu.VMEM((4, width, 2, rows, cols), f32),
            pltpu.VMEM((4, width + 1, 2, 2, rows, cols), f32),
            pltpu.VMEM((4, width + 1, 2, 2, rows, cols), f32),
            pltpu.VMEM((2, 2, width, rows, cols), f32),
            pltpu.VMEM((tx_max, width * rows), f32),
            pltpu.VMEM((tx_max, cols), f32),
            pltpu.VMEM((width, rows, cols), f32),
            pltpu.VMEM((2, freqs, 2, inner_count, share, cols), f32),
            pltpu.VMEM((2, freqs, 2, inner_count, share, cols), f32),
            pltpu.SemaphoreType.DMA((7,)),
            pltpu.SemaphoreType.DMA((2,)),
            pltpu.SemaphoreType.DMA((4, 2, 3)),
            pltpu.SemaphoreType.DMA((4, 2, 3)),
            pltpu.SemaphoreType.DMA((2, freqs)),
            pltpu.SemaphoreType.DMA((2, freqs)),
        ],
        compiler_params=pltpu.CompilerParams(
            collective_id=0, has_side_effects=True, vmem_limit_bytes=(64 * 1024 - 64) * 1024
        ),
    )(sigma_h, sigma_v, wave_scale, field_start, adjoint_start, observed, tx_count, tx_cells)


def solution(mesh):
    placed = (
        P("gx", None, None),
        P("gx", None, None),
        P("freq"),
        P("freq", None, None, "gx", None, None),
        P("freq", None, None, "gx", None, None),
        P("freq", None, None, "gx", None, None),
        P(),
        P(),
    )
    return jax.shard_map(
        functools.partial(on_device, mesh.shape["freq"], mesh.shape["gx"]),
        mesh=mesh,
        in_specs=placed,
        out_specs=(P(None, "gx", "freq", None), P("freq", None, None, "gx", None, None)),
        check_vma=False,
    )
```

```python
import functools

import jax
import jax.numpy as jnp
from jax import lax
from jax.experimental import pallas as pl
from jax.experimental.pallas import tpu as pltpu
from jax.sharding import PartitionSpec as P

THETA = 0.5
SOURCE_GAIN = 8.0
MESH = pl.DeviceIdType.MESH
E0, E1, A0, A1 = 0, 1, 2, 3


def sweeps_kernel(
    freqs, slabs, tx_max,
    sig_h_in, sig_v_in, wave, field_in, adjoint_in, observed_in, tx_count, tx_cells,
    grad_hbm, field_hbm,
    grad_out, field, sig_h, sig_v, field_start, adjoint_start, observed,
    xs, yz, gs, coef, onehot_row, onehot_z, counts, grad_send, grad_recv,
    load_sem, store_sem, halo_send, halo_recv, peer_send, peer_recv,
):
    width, rows, cols = sig_h.shape
    share = rows // freqs
    last = width - 1
    half = rows // 2
    early = half - 8
    whole = (0, rows)
    low = half // 2
    cut = {
        E0: ((early, 0), (early - 8, 0)),
        E1: ((early, 0), (early, 0)),
        A0: ((early, 0), (early, 0)),
        A1: ((half, low, 0), (early, low - 8, 0)),
    }
    me_f = lax.axis_index("freq")
    me_x = lax.axis_index("gx")
    has_left = me_x > 0
    has_right = me_x < slabs - 1
    scale = wave[0]

    def up_y(v, top):
        moved = pltpu.roll(v, v.shape[0] - 1, 0)
        if not top:
            return moved
        row_id = lax.broadcasted_iota(jnp.int32, v.shape, 0)
        return jnp.where(row_id == v.shape[0] - 1, 0.0, moved)

    def down_y(v, bottom):
        moved = pltpu.roll(v, 1, 0)
        if not bottom:
            return moved
        return jnp.where(lax.broadcasted_iota(jnp.int32, v.shape, 0) == 0, 0.0, moved)

    def up_z(v):
        col_id = lax.broadcasted_iota(jnp.int32, v.shape, 1)
        return jnp.where(col_id == cols - 1, 0.0, pltpu.roll(v, cols - 1, 1))

    def down_z(v):
        col_id = lax.broadcasted_iota(jnp.int32, v.shape, 1)
        return jnp.where(col_id == 0, 0.0, pltpu.roll(v, 1, 1))

    def put(s, i, r, part, vx, vy, vz):
        lo, hi = part
        xs[s, i, r, lo:hi] = vx
        yz[s, i, 0, r, lo:hi] = vy
        yz[s, i, 1, r, lo:hi] = vz
        if hi == rows:
            above = up_y(vx, True)
        else:
            above = up_y(xs[s, i, r, lo:hi + 8], False)[:hi - lo]
        gs[s, i + 1, 0, r, lo:hi] = vy + (above - vx)
        gs[s, i + 1, 1, r, lo:hi] = vz + (up_z(vx) - vx)

    def fill(s, i, start):
        for r in range(2):
            put(s, i, r, whole, *(start[r, c, i].astype(jnp.float32) for c in range(3)))

    def left_end(s, part):
        lo, hi = part

        @pl.when(jnp.logical_not(has_left))
        def _():
            gs[s, 0, :, :, lo:hi] = yz[s, 0, :, :, lo:hi]

    def curl(s, i, r, part):
        lo, hi = part
        w0, w1 = max(lo - 8, 0), min(hi + 8, rows)

        def crop(v):
            return v[lo - w0:hi - w0]

        vx = xs[s, i, r, lo:hi]
        wide_y, wide_z = yz[s, i, 0, r, w0:w1], yz[s, i, 1, r, w0:w1]
        hx = (up_y(wide_z, w1 == rows) - wide_z) - (up_z(wide_y) - wide_y)
        hz = yz[s, i + 1, 0, r, w0:w1] - gs[s, i + 1, 0, r, w0:w1]
        hy = gs[s, i + 1, 1, r, lo:hi] - yz[s, i + 1, 1, r, lo:hi]
        vy, vz = crop(wide_y), crop(wide_z)
        hy_before = gs[s, i, 1, r, lo:hi] - vz
        hz_before = vy - gs[s, i, 0, r, lo:hi]
        hx_c, hz_c = crop(hx), crop(hz)
        kx = (hz_c - crop(down_y(hz, w0 == 0))) - (hy - down_z(hy))
        ky = (hx_c - down_z(hx_c)) - (hz_c - hz_before)
        kz = (hy - hy_before) - (hx_c - crop(down_y(hx, w0 == 0)))
        return (vx, vy, vz), (kx, ky, kz)

    def update(s, i, rhs, part):
        lo, hi = part
        real, k_real = curl(s, i, 0, part)
        imag, k_imag = curl(s, i, 1, part)
        out_re, out_im = [], []
        for c in range(3):
            which = 1 if c == 2 else 0
            coupling = scale * (sig_v if which else sig_h)[i, lo:hi]
            main, cross = coef[which, 0, i, lo:hi], coef[which, 1, i, lo:hi]
            b_re, b_im = rhs(c, i, part)
            r_re = b_re - (k_real[c] - coupling * imag[c])
            r_im = b_im - (k_imag[c] + coupling * real[c])
            out_re.append(real[c] + (main * r_re + cross * r_im))
            out_im.append(imag[c] + (main * r_im - cross * r_re))
        return out_re, out_im

    def source(c, i, part):
        lo, hi = part
        return 0.0, (SOURCE_GAIN * scale) * counts[i, lo:hi] if c == 0 else 0.0

    def misfit(c, i, part):
        lo, hi = part
        from_row = lo // 16 * 16
        to_row = (hi + 15) // 16 * 16
        seen = [
            observed[r, c, i, from_row:to_row].astype(jnp.float32)[lo - from_row:hi - from_row]
            for r in range(2)
        ]
        return field[0, c, i, lo:hi] - seen[0], seen[1] - field[1, c, i, lo:hi]

    def advance(s, i, rhs, part=whole):
        out_re, out_im = update(s, i, rhs, part)
        put(s + 1, i, 0, part, *out_re)
        put(s + 1, i, 1, part, *out_im)

    def finish_field(i, part=whole):
        lo, hi = part
        out_re, out_im = update(E1, i, source, part)
        for c in range(3):
            field[0, c, i, lo:hi] = out_re[c]
            field[1, c, i, lo:hi] = out_im[c]

    def finish_grad(i, phase, slot, part=whole):
        lo, hi = part
        out_re, out_im = update(A1, i, misfit, part)
        terms = [
            scale * (out_re[c] * field[1, c, i, lo:hi] + out_im[c] * field[0, c, i, lo:hi])
            for c in range(3)
        ]
        for which, term in enumerate((terms[0] + terms[1], terms[2])):
            for f in range(lo // share, hi // share):
                at = f * share - lo
                grad_send[phase, f, which, slot] = term[at:at + share]

    def piece(s, way, k):
        edges = (rows,) + cut[s][way]
        return pl.ds(edges[k + 1], edges[k] - edges[k + 1])

    def rightward(s, k):
        at = piece(s, 0, k)
        return pltpu.make_async_remote_copy(
            gs.at[s, width, :, :, at], gs.at[s, 0, :, :, at],
            halo_send.at[s, 0, k], halo_recv.at[s, 0, k],
            device_id={"gx": me_x + 1}, device_id_type=MESH,
        )

    def leftward(s, k):
        at = piece(s, 1, k)
        return pltpu.make_async_remote_copy(
            yz.at[s, 0, :, :, at], yz.at[s, width, :, :, at],
            halo_send.at[s, 1, k], halo_recv.at[s, 1, k],
            device_id={"gx": me_x - 1}, device_id_type=MESH,
        )

    def send_right(s, k):
        pl.when(has_right)(lambda: rightward(s, k).start())

    def send_left(s, k):
        pl.when(has_left)(lambda: leftward(s, k).start())

    def wait_left(s, k):
        pl.when(has_left)(lambda: rightward(s, k).wait_recv())

    def wait_right(s, k):
        pl.when(has_right)(lambda: leftward(s, k).wait_recv())

    def to_peer(phase, off):
        peer = lax.rem(me_f + off, freqs)
        return pltpu.make_async_remote_copy(
            grad_send.at[phase, peer], grad_recv.at[phase, off],
            peer_send.at[phase, off], peer_recv.at[phase, off],
            device_id={"freq": peer}, device_id_type=MESH,
        )

    def inner(body):
        if width > 2:
            lax.fori_loop(1, last, lambda i, _: (body(i), 0)[1], 0)

    loads = [
        pltpu.make_async_copy(src, dst, load_sem.at[n])
        for n, (src, dst) in enumerate((
            (field_in.at[0, :, :, 0], field_start.at[:, :, 0]),
            (field_in.at[0, :, :, last], field_start.at[:, :, last]),
            (field_in.at[0, :, :, pl.ds(1, last - 1)], field_start.at[:, :, pl.ds(1, last - 1)]),
            (sig_h_in, sig_h),
            (sig_v_in, sig_v),
            (adjoint_in.at[0], adjoint_start),
            (observed_in.at[0], observed),
        ))
    ]
    for load in loads:
        load.start()
    barrier = pltpu.get_barrier_semaphore()

    @pl.when(has_left)
    def _():
        pl.semaphore_signal(barrier, 1, device_id={"gx": me_x - 1}, device_id_type=MESH)

    @pl.when(has_right)
    def _():
        pl.semaphore_signal(barrier, 1, device_id={"gx": me_x + 1}, device_id_type=MESH)

    for off in range(1, freqs):
        pl.semaphore_signal(
            barrier, 1, device_id={"freq": lax.rem(me_f + off, freqs)}, device_id_type=MESH
        )
    loads[0].wait()
    fill(E0, 0, field_start)
    loads[1].wait()
    fill(E0, last, field_start)
    pl.semaphore_wait(
        barrier, freqs - 1 + has_left.astype(jnp.int32) + has_right.astype(jnp.int32)
    )
    for k in range(2):
        send_left(E0, k)
        send_right(E0, k)

    @pl.when(jnp.logical_not(has_right))
    def _():
        for s in (E0, E1, A0, A1):
            yz[s, width] = jnp.zeros((2, 2, rows, cols), jnp.float32)

    left_end(E0, whole)
    for load in loads[2:]:
        load.wait()
    fill(A0, 0, adjoint_start)
    fill(A0, last, adjoint_start)
    for k in range(2):
        send_left(A0, k)
        send_right(A0, k)
    left_end(A0, whole)

    def prepare(i):
        for which, sig in enumerate((sig_h, sig_v)):
            coupling = scale * sig[i]
            part = THETA / (16.0 + coupling * coupling)
            coef[which, 0, i] = 4.0 * part
            coef[which, 1, i] = coupling * part

    lax.fori_loop(0, width, lambda i, _: (prepare(i), 0)[1], 0)

    row_line = lax.broadcasted_iota(jnp.int32, (1, width * rows), 1)
    col_line = lax.broadcasted_iota(jnp.int32, (1, cols), 1)

    def mark(t, _):
        cell = tx_cells[t]
        row = cell // cols
        col = cell - row * cols
        row = jnp.where(t < tx_count[0], row - me_x * (width * rows), -1)
        onehot_row[pl.ds(t, 1), :] = jnp.where(row_line == row, 1.0, 0.0)
        onehot_z[pl.ds(t, 1), :] = jnp.where(col_line == col, 1.0, 0.0)
        return 0

    lax.fori_loop(0, tx_max, mark, 0)
    counts[...] = lax.dot_general(
        onehot_row[...].astype(jnp.bfloat16), onehot_z[...].astype(jnp.bfloat16),
        (((0,), (0,)), ((), ())), preferred_element_type=jnp.float32,
    ).reshape(width, rows, cols)

    inner(lambda i: fill(E0, i, field_start))
    inner(lambda i: fill(A0, i, adjoint_start))
    inner(lambda i: advance(E0, i, source))

    for k, part in enumerate(((early, rows), (0, early))):
        wait_left(E0, k)
        advance(E0, 0, source, part)
        send_left(E1, k)
        left_end(E1, part)
        wait_right(E0, k)
        advance(E0, last, source, part)
        send_right(E1, k)

    inner(finish_field)
    inner(lambda i: advance(A0, i, misfit))

    for k, (near, far) in enumerate((((early, rows), (half, rows)), ((0, early), (0, half)))):
        wait_left(E1, k)
        finish_field(0, near)
        wait_left(A0, k)
        advance(A0, 0, misfit, near)
        for n in ((0,), (1, 2))[k]:
            send_left(A1, n)
        left_end(A1, near)
        wait_right(E1, k)
        finish_field(last, far)
        wait_right(A0, k)
        advance(A0, last, misfit, far)
        for n in ((0,), (1, 2))[k]:
            send_right(A1, n)

    store_field = pltpu.make_async_copy(field, field_hbm.at[0], store_sem.at[0])
    store_field.start()
    if width > 2:
        lax.fori_loop(1, last, lambda i, _: (finish_grad(i, 0, i - 1), 0)[1], 0)
    for off in range(1, freqs):
        to_peer(0, off).start()
    for k, part in enumerate(((half, rows), (low, half), (0, low))):
        wait_left(A1, k)
        finish_grad(0, 1, 0, part)
        wait_right(A1, k)
        finish_grad(last, 1, 1, part)
        for off in range(1, freqs):
            row = lax.rem(me_f + off, freqs) * share
            pl.when(jnp.logical_and(row >= part[0], row < part[1]))(
                lambda: to_peer(1, off).start()
            )

    for phase, layers in ((0, tuple(range(1, last))), (1, (0, last))):
        total = grad_send[phase, me_f]
        for off in range(1, freqs):
            to_peer(phase, off).wait_recv()
            total = total + grad_recv[phase, off]
        for slot, layer in enumerate(layers):
            grad_out[:, layer] = total[:, slot]
    store_grad = pltpu.make_async_copy(grad_out, grad_hbm, store_sem.at[1])
    store_grad.start()
    for off in range(1, freqs):
        to_peer(0, off).wait_send()
        to_peer(1, off).wait_send()
    for s in (E0, E1, A0, A1):
        for k in range(len(cut[s][0])):
            pl.when(has_right)(lambda: rightward(s, k).wait_send())
            pl.when(has_left)(lambda: leftward(s, k).wait_send())
    store_field.wait()
    store_grad.wait()


def hand_over_kernel(grad_in, field_in, grad_out, field_out, grad, field, sems):
    places = [(field_in.at[0, r, c], field.at[r, c], field_out.at[0, r, c]) for r in range(2) for c in range(3)]
    places += [(grad_in.at[n], grad.at[n], grad_out.at[n]) for n in range(2)]
    reads = [pltpu.make_async_copy(a, b, sems.at[0, n]) for n, (a, b, _) in enumerate(places)]
    writes = [pltpu.make_async_copy(b, c, sems.at[1, n]) for n, (_, b, c) in enumerate(places)]
    for read in reads:
        read.start()
    for read, write in zip(reads, writes):
        read.wait()
        write.start()
    for write in writes:
        write.wait()


def on_device(freqs, slabs, sigma_h, sigma_v, wave_scale, field_start, adjoint_start, observed, tx_count, tx_cells):
    width, rows, cols = sigma_h.shape
    tx_max = tx_cells.shape[0]
    share = rows // freqs
    inner_count = max(width - 2, 2)
    hbm = pl.BlockSpec(memory_space=pltpu.HBM)
    smem = pl.BlockSpec(memory_space=pltpu.SMEM)
    f32 = jnp.float32
    grad, field = pl.pallas_call(
        functools.partial(sweeps_kernel, freqs, slabs, tx_max),
        out_shape=(
            jax.ShapeDtypeStruct((2, width, share, cols), f32),
            jax.ShapeDtypeStruct(field_start.shape, f32),
        ),
        in_specs=[hbm, hbm, smem, hbm, hbm, hbm, smem, smem],
        out_specs=(hbm, hbm),
        scratch_shapes=[
            pltpu.VMEM((2, width, share, cols), f32),
            pltpu.VMEM(field_start.shape[1:], f32),
            pltpu.VMEM(sigma_h.shape, f32),
            pltpu.VMEM(sigma_v.shape, f32),
            pltpu.VMEM(field_start.shape[1:], field_start.dtype),
            pltpu.VMEM(adjoint_start.shape[1:], adjoint_start.dtype),
            pltpu.VMEM(observed.shape[1:], observed.dtype),
            pltpu.VMEM((4, width, 2, rows, cols), f32),
            pltpu.VMEM((4, width + 1, 2, 2, rows, cols), f32),
            pltpu.VMEM((4, width + 1, 2, 2, rows, cols), f32),
            pltpu.VMEM((2, 2, width, rows, cols), f32),
            pltpu.VMEM((tx_max, width * rows), f32),
            pltpu.VMEM((tx_max, cols), f32),
            pltpu.VMEM((width, rows, cols), f32),
            pltpu.VMEM((2, freqs, 2, inner_count, share, cols), f32),
            pltpu.VMEM((2, freqs, 2, inner_count, share, cols), f32),
            pltpu.SemaphoreType.DMA((7,)),
            pltpu.SemaphoreType.DMA((2,)),
            pltpu.SemaphoreType.DMA((4, 2, 3)),
            pltpu.SemaphoreType.DMA((4, 2, 3)),
            pltpu.SemaphoreType.DMA((2, freqs)),
            pltpu.SemaphoreType.DMA((2, freqs)),
        ],
        compiler_params=pltpu.CompilerParams(
            collective_id=0, has_side_effects=True, vmem_limit_bytes=(64 * 1024 - 64) * 1024
        ),
    )(sigma_h, sigma_v, wave_scale, field_start, adjoint_start, observed, tx_count, tx_cells)
    return pl.pallas_call(
        hand_over_kernel,
        out_shape=(jax.ShapeDtypeStruct(grad.shape, f32), jax.ShapeDtypeStruct(field.shape, f32)),
        in_specs=[hbm, hbm],
        out_specs=(hbm, hbm),
        scratch_shapes=[
            pltpu.VMEM(grad.shape, f32),
            pltpu.VMEM(field.shape[1:], f32),
            pltpu.SemaphoreType.DMA((2, 8)),
        ],
        compiler_params=pltpu.CompilerParams(vmem_limit_bytes=(64 * 1024 - 64) * 1024),
    )(grad, field)


def solution(mesh):
    placed = (
        P("gx", None, None),
        P("gx", None, None),
        P("freq"),
        P("freq", None, None, "gx", None, None),
        P("freq", None, None, "gx", None, None),
        P("freq", None, None, "gx", None, None),
        P(),
        P(),
    )
    return jax.shard_map(
        functools.partial(on_device, mesh.shape["freq"], mesh.shape["gx"]),
        mesh=mesh,
        in_specs=placed,
        out_specs=(P(None, "gx", "freq", None), P("freq", None, None, "gx", None, None)),
        check_vma=False,
    )
```

```python
import functools

import jax
import jax.numpy as jnp
from jax import lax
from jax.experimental import pallas as pl
from jax.experimental.pallas import tpu as pltpu
from jax.sharding import PartitionSpec as P

THETA = 0.5
SOURCE_GAIN = 8.0
MESH = pl.DeviceIdType.MESH
E0, E1, A0, A1 = 0, 1, 2, 3


def sweeps_kernel(
    freqs, slabs, tx_max,
    sig_h_in, sig_v_in, wave, field_in, adjoint_in, observed_in, tx_count, tx_cells,
    grad_hbm, field_hbm,
    grad_out, field, sig_h, sig_v, field_start, adjoint_start, observed,
    xs, yz, gs, coef, onehot_row, onehot_z, counts, grad_send, grad_recv,
    load_sem, store_sem, halo_send, halo_recv, peer_send, peer_recv,
):
    width, rows, cols = sig_h.shape
    share = rows // freqs
    last = width - 1
    half = rows // 2
    early = half - 8
    whole = (0, rows)
    low = half // 2
    cut = {
        E0: ((early, 0), (early - 8, 0)),
        E1: ((early, 0), (early, 0)),
        A0: ((early, 0), (early, 0)),
        A1: ((half, low, 0), (early, low - 8, 0)),
    }
    me_f = lax.axis_index("freq")
    me_x = lax.axis_index("gx")
    has_left = me_x > 0
    has_right = me_x < slabs - 1
    scale = wave[0]

    def up_y(v, top):
        moved = pltpu.roll(v, v.shape[0] - 1, 0)
        if not top:
            return moved
        row_id = lax.broadcasted_iota(jnp.int32, v.shape, 0)
        return jnp.where(row_id == v.shape[0] - 1, 0.0, moved)

    def down_y(v, bottom):
        moved = pltpu.roll(v, 1, 0)
        if not bottom:
            return moved
        return jnp.where(lax.broadcasted_iota(jnp.int32, v.shape, 0) == 0, 0.0, moved)

    def up_z(v):
        col_id = lax.broadcasted_iota(jnp.int32, v.shape, 1)
        return jnp.where(col_id == cols - 1, 0.0, pltpu.roll(v, cols - 1, 1))

    def down_z(v):
        col_id = lax.broadcasted_iota(jnp.int32, v.shape, 1)
        return jnp.where(col_id == 0, 0.0, pltpu.roll(v, 1, 1))

    def put(s, i, r, part, vx, vy, vz):
        lo, hi = part
        xs[s, i, r, lo:hi] = vx
        yz[s, i, 0, r, lo:hi] = vy
        yz[s, i, 1, r, lo:hi] = vz
        if hi == rows:
            above = up_y(vx, True)
        else:
            above = up_y(xs[s, i, r, lo:hi + 8], False)[:hi - lo]
        gs[s, i + 1, 0, r, lo:hi] = vy + (above - vx)
        gs[s, i + 1, 1, r, lo:hi] = vz + (up_z(vx) - vx)

    def fill(s, i, start):
        for r in range(2):
            put(s, i, r, whole, *(start[r, c, i].astype(jnp.float32) for c in range(3)))

    def left_end(s, part):
        lo, hi = part

        @pl.when(jnp.logical_not(has_left))
        def _():
            gs[s, 0, :, :, lo:hi] = yz[s, 0, :, :, lo:hi]

    def curl(s, i, r, part):
        lo, hi = part
        w0, w1 = max(lo - 8, 0), min(hi + 8, rows)

        def crop(v):
            return v[lo - w0:hi - w0]

        vx = xs[s, i, r, lo:hi]
        wide_y, wide_z = yz[s, i, 0, r, w0:w1], yz[s, i, 1, r, w0:w1]
        hx = (up_y(wide_z, w1 == rows) - wide_z) - (up_z(wide_y) - wide_y)
        hz = yz[s, i + 1, 0, r, w0:w1] - gs[s, i + 1, 0, r, w0:w1]
        hy = gs[s, i + 1, 1, r, lo:hi] - yz[s, i + 1, 1, r, lo:hi]
        vy, vz = crop(wide_y), crop(wide_z)
        hy_before = gs[s, i, 1, r, lo:hi] - vz
        hz_before = vy - gs[s, i, 0, r, lo:hi]
        hx_c, hz_c = crop(hx), crop(hz)
        kx = (hz_c - crop(down_y(hz, w0 == 0))) - (hy - down_z(hy))
        ky = (hx_c - down_z(hx_c)) - (hz_c - hz_before)
        kz = (hy - hy_before) - (hx_c - crop(down_y(hx, w0 == 0)))
        return (vx, vy, vz), (kx, ky, kz)

    def update(s, i, rhs, part):
        lo, hi = part
        real, k_real = curl(s, i, 0, part)
        imag, k_imag = curl(s, i, 1, part)
        out_re, out_im = [], []
        for c in range(3):
            which = 1 if c == 2 else 0
            coupling = scale * (sig_v if which else sig_h)[i, lo:hi]
            main, cross = coef[which, 0, i, lo:hi], coef[which, 1, i, lo:hi]
            b_re, b_im = rhs(c, i, part)
            r_re = b_re - (k_real[c] - coupling * imag[c])
            r_im = b_im - (k_imag[c] + coupling * real[c])
            out_re.append(real[c] + (main * r_re + cross * r_im))
            out_im.append(imag[c] + (main * r_im - cross * r_re))
        return out_re, out_im

    def source(c, i, part):
        lo, hi = part
        return 0.0, (SOURCE_GAIN * scale) * counts[i, lo:hi] if c == 0 else 0.0

    def misfit(c, i, part):
        lo, hi = part
        from_row = lo // 16 * 16
        to_row = (hi + 15) // 16 * 16
        seen = [
            observed[r, c, i, from_row:to_row].astype(jnp.float32)[lo - from_row:hi - from_row]
            for r in range(2)
        ]
        return field[0, c, i, lo:hi] - seen[0], seen[1] - field[1, c, i, lo:hi]

    def advance(s, i, rhs, part=whole):
        out_re, out_im = update(s, i, rhs, part)
        put(s + 1, i, 0, part, *out_re)
        put(s + 1, i, 1, part, *out_im)

    def finish_field(i, part=whole):
        lo, hi = part
        out_re, out_im = update(E1, i, source, part)
        for c in range(3):
            field[0, c, i, lo:hi] = out_re[c]
            field[1, c, i, lo:hi] = out_im[c]

    def finish_grad(i, phase, slot, part=whole):
        lo, hi = part
        out_re, out_im = update(A1, i, misfit, part)
        terms = [
            scale * (out_re[c] * field[1, c, i, lo:hi] + out_im[c] * field[0, c, i, lo:hi])
            for c in range(3)
        ]
        for which, term in enumerate((terms[0] + terms[1], terms[2])):
            for f in range(lo // share, hi // share):
                at = f * share - lo
                grad_send[phase, f, which, slot] = term[at:at + share]

    def piece(s, way, k):
        edges = (rows,) + cut[s][way]
        return pl.ds(edges[k + 1], edges[k] - edges[k + 1])

    def rightward(s, k):
        at = piece(s, 0, k)
        return pltpu.make_async_remote_copy(
            gs.at[s, width, :, :, at], gs.at[s, 0, :, :, at],
            halo_send.at[s, 0, k], halo_recv.at[s, 0, k],
            device_id={"gx": me_x + 1}, device_id_type=MESH,
        )

    def leftward(s, k):
        at = piece(s, 1, k)
        return pltpu.make_async_remote_copy(
            yz.at[s, 0, :, :, at], yz.at[s, width, :, :, at],
            halo_send.at[s, 1, k], halo_recv.at[s, 1, k],
            device_id={"gx": me_x - 1}, device_id_type=MESH,
        )

    def send_right(s, k):
        pl.when(has_right)(lambda: rightward(s, k).start())

    def send_left(s, k):
        pl.when(has_left)(lambda: leftward(s, k).start())

    def wait_left(s, k):
        pl.when(has_left)(lambda: rightward(s, k).wait_recv())

    def wait_right(s, k):
        pl.when(has_right)(lambda: leftward(s, k).wait_recv())

    def to_peer(phase, off):
        peer = lax.rem(me_f + off, freqs)
        return pltpu.make_async_remote_copy(
            grad_send.at[phase, peer], grad_recv.at[phase, off],
            peer_send.at[phase, off], peer_recv.at[phase, off],
            device_id={"freq": peer}, device_id_type=MESH,
        )

    def inner(body):
        if width > 2:
            lax.fori_loop(1, last, lambda i, _: (body(i), 0)[1], 0)

    loads = [
        pltpu.make_async_copy(src, dst, load_sem.at[n])
        for n, (src, dst) in enumerate((
            (field_in.at[0, :, :, 0], field_start.at[:, :, 0]),
            (field_in.at[0, :, :, last], field_start.at[:, :, last]),
            (adjoint_in.at[0], adjoint_start),
            (sig_h_in, sig_h),
            (sig_v_in, sig_v),
            (field_in.at[0, :, :, pl.ds(1, last - 1)], field_start.at[:, :, pl.ds(1, last - 1)]),
            (observed_in.at[0], observed),
        ))
    ]
    for load in loads:
        load.start()
    barrier = pltpu.get_barrier_semaphore()

    @pl.when(has_left)
    def _():
        pl.semaphore_signal(barrier, 1, device_id={"gx": me_x - 1}, device_id_type=MESH)

    @pl.when(has_right)
    def _():
        pl.semaphore_signal(barrier, 1, device_id={"gx": me_x + 1}, device_id_type=MESH)

    for off in range(1, freqs):
        pl.semaphore_signal(
            barrier, 1, device_id={"freq": lax.rem(me_f + off, freqs)}, device_id_type=MESH
        )
    loads[0].wait()
    fill(E0, 0, field_start)
    loads[1].wait()
    fill(E0, last, field_start)
    pl.semaphore_wait(
        barrier, freqs - 1 + has_left.astype(jnp.int32) + has_right.astype(jnp.int32)
    )
    for k in range(2):
        send_left(E0, k)
        send_right(E0, k)

    @pl.when(jnp.logical_not(has_right))
    def _():
        for s in (E0, E1, A0, A1):
            yz[s, width] = jnp.zeros((2, 2, rows, cols), jnp.float32)

    left_end(E0, whole)
    loads[2].wait()
    fill(A0, 0, adjoint_start)
    fill(A0, last, adjoint_start)
    for k in range(2):
        send_left(A0, k)
        send_right(A0, k)
    left_end(A0, whole)
    for load in loads[3:]:
        load.wait()

    def prepare(i):
        for which, sig in enumerate((sig_h, sig_v)):
            coupling = scale * sig[i]
            part = THETA / (16.0 + coupling * coupling)
            coef[which, 0, i] = 4.0 * part
            coef[which, 1, i] = coupling * part

    lax.fori_loop(0, width, lambda i, _: (prepare(i), 0)[1], 0)

    row_line = lax.broadcasted_iota(jnp.int32, (1, width * rows), 1)
    col_line = lax.broadcasted_iota(jnp.int32, (1, cols), 1)

    def mark(t, _):
        cell = tx_cells[t]
        row = cell // cols
        col = cell - row * cols
        row = jnp.where(t < tx_count[0], row - me_x * (width * rows), -1)
        onehot_row[pl.ds(t, 1), :] = jnp.where(row_line == row, 1.0, 0.0)
        onehot_z[pl.ds(t, 1), :] = jnp.where(col_line == col, 1.0, 0.0)
        return 0

    lax.fori_loop(0, tx_max, mark, 0)
    counts[...] = lax.dot_general(
        onehot_row[...].astype(jnp.bfloat16), onehot_z[...].astype(jnp.bfloat16),
        (((0,), (0,)), ((), ())), preferred_element_type=jnp.float32,
    ).reshape(width, rows, cols)

    inner(lambda i: fill(E0, i, field_start))
    inner(lambda i: fill(A0, i, adjoint_start))
    inner(lambda i: advance(E0, i, source))

    for k, part in enumerate(((early, rows), (0, early))):
        wait_left(E0, k)
        advance(E0, 0, source, part)
        send_left(E1, k)
        left_end(E1, part)
        wait_right(E0, k)
        advance(E0, last, source, part)
        send_right(E1, k)

    inner(finish_field)
    inner(lambda i: advance(A0, i, misfit))

    for k, (near, far) in enumerate((((early, rows), (half, rows)), ((0, early), (0, half)))):
        wait_left(E1, k)
        finish_field(0, near)
        wait_left(A0, k)
        advance(A0, 0, misfit, near)
        for n in ((0,), (1, 2))[k]:
            send_left(A1, n)
        left_end(A1, near)
        wait_right(E1, k)
        finish_field(last, far)
        wait_right(A0, k)
        advance(A0, last, misfit, far)
        for n in ((0,), (1, 2))[k]:
            send_right(A1, n)

    store_field = pltpu.make_async_copy(field, field_hbm.at[0], store_sem.at[0])
    store_field.start()
    if width > 2:
        lax.fori_loop(1, last, lambda i, _: (finish_grad(i, 0, i - 1), 0)[1], 0)
    for off in range(1, freqs):
        to_peer(0, off).start()
    def gather(phase, layers):
        total = grad_send[phase, me_f]
        for off in range(1, freqs):
            to_peer(phase, off).wait_recv()
            total = total + grad_recv[phase, off]
        for slot, layer in enumerate(layers):
            grad_out[:, layer] = total[:, slot]

    for k, part in enumerate(((half, rows), (low, half), (0, low))):
        if k == 2:
            gather(0, tuple(range(1, last)))
        wait_left(A1, k)
        finish_grad(0, 1, 0, part)
        wait_right(A1, k)
        finish_grad(last, 1, 1, part)
        for off in range(1, freqs):
            row = lax.rem(me_f + off, freqs) * share
            pl.when(jnp.logical_and(row >= part[0], row < part[1]))(
                lambda: to_peer(1, off).start()
            )

    gather(1, (0, last))
    store_grad = pltpu.make_async_copy(grad_out, grad_hbm, store_sem.at[1])
    store_grad.start()
    for off in range(1, freqs):
        to_peer(0, off).wait_send()
        to_peer(1, off).wait_send()
    for s in (E0, E1, A0, A1):
        for k in range(len(cut[s][0])):
            pl.when(has_right)(lambda: rightward(s, k).wait_send())
            pl.when(has_left)(lambda: leftward(s, k).wait_send())
    store_field.wait()
    store_grad.wait()


def hand_over_kernel(grad_in, field_in, grad_out, field_out, grad, field, sems):
    places = [(field_in.at[0, r, c], field.at[r, c], field_out.at[0, r, c]) for r in range(2) for c in range(3)]
    places += [(grad_in.at[n], grad.at[n], grad_out.at[n]) for n in range(2)]
    reads = [pltpu.make_async_copy(a, b, sems.at[0, n]) for n, (a, b, _) in enumerate(places)]
    writes = [pltpu.make_async_copy(b, c, sems.at[1, n]) for n, (_, b, c) in enumerate(places)]
    for read in reads:
        read.start()
    for read, write in zip(reads, writes):
        read.wait()
        write.start()
    for write in writes:
        write.wait()


def on_device(freqs, slabs, sigma_h, sigma_v, wave_scale, field_start, adjoint_start, observed, tx_count, tx_cells):
    width, rows, cols = sigma_h.shape
    tx_max = tx_cells.shape[0]
    share = rows // freqs
    inner_count = max(width - 2, 2)
    hbm = pl.BlockSpec(memory_space=pltpu.HBM)
    smem = pl.BlockSpec(memory_space=pltpu.SMEM)
    f32 = jnp.float32
    grad, field = pl.pallas_call(
        functools.partial(sweeps_kernel, freqs, slabs, tx_max),
        out_shape=(
            jax.ShapeDtypeStruct((2, width, share, cols), f32),
            jax.ShapeDtypeStruct(field_start.shape, f32),
        ),
        in_specs=[hbm, hbm, smem, hbm, hbm, hbm, smem, smem],
        out_specs=(hbm, hbm),
        scratch_shapes=[
            pltpu.VMEM((2, width, share, cols), f32),
            pltpu.VMEM(field_start.shape[1:], f32),
            pltpu.VMEM(sigma_h.shape, f32),
            pltpu.VMEM(sigma_v.shape, f32),
            pltpu.VMEM(field_start.shape[1:], field_start.dtype),
            pltpu.VMEM(adjoint_start.shape[1:], adjoint_start.dtype),
            pltpu.VMEM(observed.shape[1:], observed.dtype),
            pltpu.VMEM((4, width, 2, rows, cols), f32),
            pltpu.VMEM((4, width + 1, 2, 2, rows, cols), f32),
            pltpu.VMEM((4, width + 1, 2, 2, rows, cols), f32),
            pltpu.VMEM((2, 2, width, rows, cols), f32),
            pltpu.VMEM((tx_max, width * rows), f32),
            pltpu.VMEM((tx_max, cols), f32),
            pltpu.VMEM((width, rows, cols), f32),
            pltpu.VMEM((2, freqs, 2, inner_count, share, cols), f32),
            pltpu.VMEM((2, freqs, 2, inner_count, share, cols), f32),
            pltpu.SemaphoreType.DMA((7,)),
            pltpu.SemaphoreType.DMA((2,)),
            pltpu.SemaphoreType.DMA((4, 2, 3)),
            pltpu.SemaphoreType.DMA((4, 2, 3)),
            pltpu.SemaphoreType.DMA((2, freqs)),
            pltpu.SemaphoreType.DMA((2, freqs)),
        ],
        compiler_params=pltpu.CompilerParams(
            collective_id=0, has_side_effects=True, vmem_limit_bytes=(64 * 1024 - 64) * 1024
        ),
    )(sigma_h, sigma_v, wave_scale, field_start, adjoint_start, observed, tx_count, tx_cells)
    return pl.pallas_call(
        hand_over_kernel,
        out_shape=(jax.ShapeDtypeStruct(grad.shape, f32), jax.ShapeDtypeStruct(field.shape, f32)),
        in_specs=[hbm, hbm],
        out_specs=(hbm, hbm),
        scratch_shapes=[
            pltpu.VMEM(grad.shape, f32),
            pltpu.VMEM(field.shape[1:], f32),
            pltpu.SemaphoreType.DMA((2, 8)),
        ],
        compiler_params=pltpu.CompilerParams(vmem_limit_bytes=(64 * 1024 - 64) * 1024),
    )(grad, field)


def solution(mesh):
    placed = (
        P("gx", None, None),
        P("gx", None, None),
        P("freq"),
        P("freq", None, None, "gx", None, None),
        P("freq", None, None, "gx", None, None),
        P("freq", None, None, "gx", None, None),
        P(),
        P(),
    )
    return jax.shard_map(
        functools.partial(on_device, mesh.shape["freq"], mesh.shape["gx"]),
        mesh=mesh,
        in_specs=placed,
        out_specs=(P(None, "gx", "freq", None), P("freq", None, None, "gx", None, None)),
        check_vma=False,
    )
```
